32 devices in a mesh: scen: 2 (over y), tm: 8 (over z, x), panel: 2 (over core).
Axes of the slice: x: 2, y: 2, z: 4, core: 2. Of those that a mesh axis runs over, the one named last changes fastest.
Arguments:
- panels: bfloat16 [16, 1024, 2048], P(('scen', 'tm'), 'panel'), parts along dimension 0, may hold values from -0.1875 to 0.1875
- barrier: bfloat16 [16, 1024], P(('scen', 'tm'), 'panel'), parts along dimension 0, may hold values from 0.099609375 to 10
- counts: int32 [16, 2], P(('scen', 'tm'), 'panel'), parts along dimension 0, may hold values from 1 to 8
Outputs:
- diag_blocks: bfloat16 [16, 1024, 1024], P(('scen', 'tm'), 'panel'), parts along dimension 0
- cross_blocks: bfloat16 [16, 1024, 1024], P(('scen', 'tm'), 'panel'), parts along dimension 0
The draws below stay inside these ranges and needn't reach their ends.
There are 2 independent parts, one for each index of `scen`. The reference program is written for one: setup_inputs(seed, part) draws one part's arguments, and reference() takes and returns one part's arrays. A program takes and returns all parts, laid end to end along the dimension named above; each array names one. Nothing has to cross between parts.
Inputs may be any that keep to these rules, and one draw needn't show every extreme that they name: The first 64 * counts[t, p] rows of group p of block t are live; every device of the panel axis has at least one live slot.
All inputs are finite; a program needn't handle non-finite values.
Results may differ from the reference program's by a relative error of at most 0.0059.
Values may be sent and summed in bfloat16 or wider, within the bound.
A program may use at most 64 MiB of HBM per device.

```python
import math
import jax
import jax.numpy as jnp
from jax import lax

B = 1024
PR = 64
SLOTS = 8
BLOCKS = 8
ROWS = 1024
N_PANEL = 2


def with_ends(entries, key, smallest, largest):
    extent = entries.shape
    spot = [jax.random.randint(jax.random.fold_in(key, axis), (), 0, extent[axis]) for axis in range(len(extent))]
    entries = entries.at[tuple(spot)].set(smallest)
    longest = extent.index(max(extent))
    spot[longest] = (spot[longest] + 1) % extent[longest]
    return entries.at[tuple(spot)].set(largest)


def block_scale(own_key, extent, shards, smallest, top_value):
    def one(position, shards_of):
        draws = jax.random.uniform(jax.random.fold_in(jax.random.fold_in(own_key, 6), position), (shards_of,), jnp.float32, smallest / len(shards), top_value / len(shards))
        return jnp.repeat(jnp.exp(draws), extent[position] // shards_of).reshape((-1,) + (1,) * (len(extent) - position - 1))

    level = one(*shards[0])
    for cut in shards[1:]:
        level = level * one(*cut)
    return level


def normal_values(own_key, shape, deviation, bound, shards=(), held_as=jnp.bfloat16):
    factor_of = block_scale(own_key, shape, shards, -0.22, 0.18) if shards else 1.0
    drawn = jax.random.normal(own_key, shape, jnp.float32) * deviation * factor_of
    return jnp.minimum(jnp.maximum(drawn, -bound), bound).astype(held_as)


def setup_inputs(seed: int = 0, part: int = 0) -> dict:
    seeds = jax.random.split(jax.random.key(seed), 4)
    part_splits = jax.random.split(jax.random.fold_in(seeds[3], part), 4)
    return {
        "panels": normal_values(part_splits[0], (BLOCKS, ROWS, 2 * B), (2 * SLOTS * PR) ** -0.5, 0.1875, ((0, 8), (1, 2))),
        "barrier": jnp.clip(jnp.exp(math.log(10.0) - 4.609084 * jax.random.uniform(part_splits[1], (BLOCKS, ROWS), jnp.float32) ** block_scale(part_splits[1], (BLOCKS, ROWS), ((0, 8), (1, 2)), -0.2, 0.2)), 0.099609375, 10.0).astype(jnp.bfloat16),
        "counts": with_ends(jax.random.randint(part_splits[2], (BLOCKS, N_PANEL), 1, SLOTS + 1), jax.random.fold_in(part_splits[2], 1), 1, SLOTS).astype(jnp.int32),
    }


def scale_rows(plain_rows, diagonal, live_count):
    live_mask = jnp.arange(plain_rows.shape[0], dtype=jnp.int32) < live_count * PR
    product = (plain_rows.astype(jnp.float32) * diagonal.astype(jnp.float32)[:, None]).astype(jnp.bfloat16)
    return jnp.where(live_mask[:, None], product, jnp.zeros_like(product))


def one_block(inputs):
    own_rows, own_diag, own_counts, early_rows, early_diag, early_counts = inputs
    group_rows = SLOTS * PR
    diag_sum = jnp.zeros((B, B), jnp.float32)
    cross_sum = jnp.zeros((B, B), jnp.float32)
    for group in range(N_PANEL):
        lower = group * group_rows
        plain_rows = own_rows[lower:lower + group_rows]
        scaled = scale_rows(plain_rows, own_diag[lower:lower + group_rows], own_counts[group])
        left_cross = jnp.dot(scaled[:, :B].T, plain_rows, preferred_element_type=jnp.float32)
        earlier_plain = early_rows[lower:lower + group_rows]
        earlier_scaled = scale_rows(earlier_plain, early_diag[lower:lower + group_rows], early_counts[group])
        right_round = jnp.dot(earlier_scaled[:, B:].T, earlier_plain[:, B:], preferred_element_type=jnp.float32).astype(jnp.bfloat16)
        right_round = lax.optimization_barrier(right_round)
        partial_diag = (left_cross[:, :B] + right_round.astype(jnp.float32)).astype(jnp.bfloat16)
        partial_diag = lax.optimization_barrier(partial_diag)
        cross_round = lax.optimization_barrier(left_cross[:, B:].astype(jnp.bfloat16))
        diag_sum = diag_sum + partial_diag.astype(jnp.float32)
        cross_sum = cross_sum + cross_round.astype(jnp.float32)
    return diag_sum.astype(jnp.bfloat16), cross_sum.astype(jnp.bfloat16)


def reference(panels, barrier, counts):
    early_rows = jnp.concatenate([jnp.zeros_like(panels[:1]), panels[:-1]], axis=0)
    early_diag = jnp.concatenate([jnp.zeros_like(barrier[:1]), barrier[:-1]], axis=0)
    early_counts = jnp.concatenate([jnp.zeros_like(counts[:1]), counts[:-1]], axis=0)
    diag_blocks, cross_blocks = lax.map(one_block, (panels, barrier, counts, early_rows, early_diag, early_counts))
    return diag_blocks, cross_blocks
```

```python
import functools

import jax
import jax.numpy as jnp
from jax import lax
from jax.experimental import pallas as pl
from jax.experimental.pallas import tpu as pltpu
from jax.sharding import PartitionSpec as P

PR = 64
MESH = pl.DeviceIdType.MESH
F32 = jnp.float32
BF16 = jnp.bfloat16
PAD = 16


def gram(left, right):
    return jnp.dot(left, right, preferred_element_type=F32)


def kernel(
    blocks,
    panels_ref,
    barrier_ref,
    counts_ref,
    diag_ref,
    cross_ref,
    rows,
    weight_row,
    weight_peer,
    weight_col,
    right_t,
    left_t,
    total,
    out_tiles,
    in_tiles,
    peer_tiles,
    local_sem,
    peer_send,
    peer_recv,
    link_send,
    link_recv,
    pass_send,
    pass_recv,
):
    R = panels_ref.shape[1]
    B = panels_ref.shape[2] // 2
    H = B // 2
    Q = H // 2
    s, t, p = lax.axis_index("scen"), lax.axis_index("tm"), lax.axis_index("panel")
    q = 1 - p
    peer = (s, t, q)
    after = (s, lax.rem(t + 1, blocks), p)
    before = (s, lax.rem(t + blocks - 1, blocks), p)
    has_before, has_after = t > 0, t < blocks - 1

    local_right = pltpu.make_async_copy(
        panels_ref.at[0, :, pl.ds(B, B)], rows.at[pl.ds(0, R), pl.ds(B, B)], local_sem.at[0]
    )
    local_left = pltpu.make_async_copy(
        panels_ref.at[0, :, pl.ds(0, B)], rows.at[pl.ds(0, R), pl.ds(0, B)], local_sem.at[1]
    )
    local_right.start()
    local_left.start()

    entry = pltpu.get_barrier_semaphore()
    pl.semaphore_signal(entry, inc=1, device_id=peer, device_id_type=MESH)

    @pl.when(has_before)
    def _():
        pl.semaphore_signal(entry, inc=1, device_id=before, device_id_type=MESH)

    @pl.when(has_after)
    def _():
        pl.semaphore_signal(entry, inc=1, device_id=after, device_id_type=MESH)

    spot = lax.broadcasted_iota(jnp.int32, (8, R), 1)
    diagonal = jnp.broadcast_to(barrier_ref[...].astype(F32), (8, R))
    weight_row[...] = jnp.where(spot < counts_ref[0, 0] * PR, diagonal, 0.0)

    def right_tile(half, tile):
        return pl.ds(pl.multiple_of(B + half * H + tile * Q, Q), Q)

    def to_peer(columns, which):
        return pltpu.make_async_remote_copy(
            src_ref=panels_ref.at[0, :, columns],
            dst_ref=rows.at[pl.ds(R, R), columns],
            send_sem=peer_send.at[which],
            recv_sem=peer_recv.at[which],
            device_id=peer,
            device_id_type=MESH,
        )

    def exchange(dest):
        rest = 1 - dest
        return [
            to_peer(right_tile(dest, 0), 0),
            to_peer(right_tile(rest, dest), 1),
            to_peer(right_tile(dest, 1), 2),
            to_peer(right_tile(rest, 1 - dest), 3),
            to_peer(pl.ds(pl.multiple_of(dest * H, H), H), 4),
            to_peer(pl.ds(pl.multiple_of(rest * H, H), H), 5),
        ]

    weight_copy = pltpu.make_async_remote_copy(
        src_ref=weight_row,
        dst_ref=weight_peer,
        send_sem=peer_send.at[6],
        recv_sem=peer_recv.at[6],
        device_id=peer,
        device_id_type=MESH,
    )
    pl.semaphore_wait(entry, 1 + has_before.astype(jnp.int32) + has_after.astype(jnp.int32))
    weight_copy.start()
    sent = exchange(q)
    came = exchange(p)
    for copy in sent:
        copy.start()

    def spread(row):
        return jnp.broadcast_to(row[0:1, :], (128, R)).T

    def scaled_t(group, columns, width):
        weight = weight_col[pl.ds(group * R, R), :]
        plain = rows[pl.ds(group * R, R), columns].astype(F32)
        weight = jnp.concatenate([weight] * (width // 128), axis=1)
        return (plain * weight).astype(BF16).T

    weight_col[pl.ds(0, R), :] = spread(weight_row[...])
    local_right.wait()
    for tile in range(2):
        right_t[pl.ds(tile * Q, Q), pl.ds(0, R)] = scaled_t(0, right_tile(p, tile), Q)
    weight_copy.wait_recv()
    weight_col[pl.ds(R, R), :] = spread(weight_peer[...])

    def link(first, length, which):
        return pltpu.make_async_remote_copy(
            src_ref=out_tiles.at[pl.ds(first, length), :],
            dst_ref=in_tiles.at[pl.ds(first, length), :],
            send_sem=link_send.at[which],
            recv_sem=link_recv.at[which],
            device_id=after,
            device_id_type=MESH,
        )

    links = [link(0, Q, 0), link(Q, Q, 1), link(2 * Q, Q, 2), link(3 * Q, Q + PAD, 3)]

    def send_on(which):
        @pl.when(has_after)
        def _():
            links[which].start()

    lower = lax.broadcasted_iota(jnp.int32, (Q, Q), 0)
    upper = lax.broadcasted_iota(jnp.int32, (Q, Q), 1)

    for tile in range(2):
        came[2 * tile].wait_recv()
        right_t[pl.ds(tile * Q, Q), pl.ds(R, R)] = scaled_t(1, right_tile(p, tile), Q)
        came[2 * tile + 1].wait_recv()
        other = lax.rem(tile + p, 2)
        out_tiles[pl.ds(tile * Q, Q), :] = gram(
            right_t[pl.ds(tile * Q, Q), :], rows[:, right_tile(q, other)]
        ).astype(BF16)
        send_on(tile)
    out_tiles[pl.ds(2 * Q, Q), :] = gram(
        right_t[pl.ds(0, Q), :], rows[:, right_tile(p, 1)]
    ).astype(BF16)
    send_on(2)
    first = gram(right_t[pl.ds(0, Q), :], rows[:, right_tile(p, 0)])
    second = gram(right_t[pl.ds(Q, Q), :], rows[:, right_tile(p, 1)])
    out_tiles[pl.ds(3 * Q, Q), :] = jnp.where(upper >= lower, first, second).astype(BF16)
    middle = jnp.sum(jnp.where(upper == lower, second, 0.0), axis=0, keepdims=True)
    out_tiles[pl.ds(4 * Q, PAD), :] = jnp.broadcast_to(middle, (PAD, Q)).astype(BF16)
    send_on(3)

    own_left = pl.ds(pl.multiple_of(p * H, H), H)
    local_left.wait()
    left_t[:, pl.ds(0, R)] = scaled_t(0, own_left, H)
    came[4].wait_recv()
    left_t[:, pl.ds(R, R)] = scaled_t(1, own_left, H)
    came[5].wait_recv()

    def left_step(step, carry):
        here = pl.ds(pl.multiple_of(step * Q, Q), Q)
        total[:, here] = gram(left_t[...], rows[:, here])
        return carry

    lax.fori_loop(0, B // Q, left_step, 0)

    def cross_step(step, carry):
        here = pl.ds(pl.multiple_of(step * Q, Q), Q)
        there = pl.ds(pl.multiple_of(B + step * Q, Q), Q)
        cross_ref[:, here] = gram(left_t[...], rows[:, there]).astype(BF16)
        return carry

    def handed(which):
        return pltpu.make_async_remote_copy(
            src_ref=in_tiles.at[pl.ds(which * Q, Q), :],
            dst_ref=peer_tiles.at[pl.ds(which * Q, Q), :],
            send_sem=pass_send.at[which],
            recv_sem=pass_recv.at[which],
            device_id=peer,
            device_id_type=MESH,
        )

    passes = [handed(0), handed(1)]

    @pl.when(has_before)
    def _():
        links[0].wait_recv()
        passes[0].start()

    lax.fori_loop(0, B // Q, cross_step, 0)

    def columns(half, tile):
        return pl.ds(pl.multiple_of(half * H + tile * Q, Q), Q)

    def band(tile):
        return pl.ds(pl.multiple_of(tile * Q, Q), Q)

    def put(row_tile, where, value):
        diag_ref[band(row_tile), where] = (total[band(row_tile), where] + value).astype(BF16)

    @pl.when(t == 0)
    def _():
        diag_ref[...] = total[...].astype(BF16)

    @pl.when(has_before)
    def _():
        put(0, columns(q, p), in_tiles[pl.ds(0, Q), :].astype(F32))
        links[1].wait_recv()
        passes[1].start()
        put(1, columns(q, 1 - p), in_tiles[pl.ds(Q, Q), :].astype(F32))
        for tile in range(2):
            passes[tile].wait_recv()
            turned = peer_tiles[pl.ds(tile * Q, Q), :].astype(F32).T
            put(lax.rem(tile + q, 2), columns(q, tile), turned)
        links[2].wait_recv()
        square = in_tiles[pl.ds(2 * Q, Q), :].astype(F32)
        put(0, columns(p, 1), square)
        put(1, columns(p, 0), square.T)
        links[3].wait_recv()
        packed = in_tiles[pl.ds(3 * Q, Q), :].astype(F32)
        turned = packed.T
        put(0, columns(p, 0), jnp.where(upper >= lower, packed, turned))
        middle_row = in_tiles[pl.ds(4 * Q, PAD), :].astype(F32)[0:1, :]
        put(
            1,
            columns(p, 1),
            jnp.where(
                upper == lower,
                jnp.broadcast_to(middle_row, (Q, Q)),
                jnp.where(upper < lower, packed, turned),
            ),
        )
        for copy in passes:
            copy.wait_send()

    weight_copy.wait_send()
    for copy in sent:
        copy.wait_send()

    @pl.when(has_after)
    def _():
        for copy in links:
            copy.wait_send()


def body(panels, barrier, counts):
    R = panels.shape[1]
    B = panels.shape[2] // 2
    H = B // 2
    Q = H // 2
    tiles = 4 * Q + PAD
    flops = 2 * 3 * H * B * 2 * R
    diag, cross = pl.pallas_call(
        functools.partial(kernel, lax.axis_size("tm")),
        out_shape=(
            jax.ShapeDtypeStruct((H, B), BF16),
            jax.ShapeDtypeStruct((H, B), BF16),
        ),
        in_specs=[
            pl.BlockSpec(memory_space=pl.ANY),
            pl.BlockSpec(memory_space=pltpu.VMEM),
            pl.BlockSpec(memory_space=pltpu.SMEM),
        ],
        out_specs=(
            pl.BlockSpec(memory_space=pltpu.VMEM),
            pl.BlockSpec(memory_space=pltpu.VMEM),
        ),
        scratch_shapes=[
            pltpu.VMEM((2 * R, 2 * B), BF16),
            pltpu.VMEM((8, R), F32),
            pltpu.VMEM((8, R), F32),
            pltpu.VMEM((2 * R, 128), F32),
            pltpu.VMEM((H, 2 * R), BF16),
            pltpu.VMEM((H, 2 * R), BF16),
            pltpu.VMEM((H, B), F32),
            pltpu.VMEM((tiles, Q), BF16),
            pltpu.VMEM((tiles, Q), BF16),
            pltpu.VMEM((2 * Q, Q), BF16),
            pltpu.SemaphoreType.DMA((2,)),
            pltpu.SemaphoreType.DMA((7,)),
            pltpu.SemaphoreType.DMA((7,)),
            pltpu.SemaphoreType.DMA((4,)),
            pltpu.SemaphoreType.DMA((4,)),
            pltpu.SemaphoreType.DMA((2,)),
            pltpu.SemaphoreType.DMA((2,)),
        ],
        compiler_params=pltpu.CompilerParams(
            collective_id=0, has_side_effects=True, vmem_limit_bytes=48 * 1024 * 1024
        ),
        cost_estimate=pl.CostEstimate(
            flops=flops, bytes_accessed=4 * R * B * 2 + 4 * H * B, transcendentals=0
        ),
    )(panels, barrier, counts)
    return diag[None], cross[None]


def solution(mesh):
    return jax.shard_map(
        body,
        mesh=mesh,
        in_specs=(
            P(("scen", "tm"), "panel", None),
            P(("scen", "tm"), "panel"),
            P(("scen", "tm"), "panel"),
        ),
        out_specs=(P(("scen", "tm"), "panel", None), P(("scen", "tm"), "panel", None)),
        check_vma=False,
    )
```

```python
import functools

import jax
import jax.numpy as jnp
from jax import lax
from jax.experimental import pallas as pl
from jax.experimental.pallas import tpu as pltpu
from jax.sharding import PartitionSpec as P

PR = 64
VMEM_BYTES = 50 * 1024 * 1024
MESH = pl.DeviceIdType.MESH
F32 = jnp.float32
BF16 = jnp.bfloat16
PAD = 16
PIECES = 4


def gram(left, right):
    return jnp.dot(left, right, preferred_element_type=F32)


def kernel(
    blocks,
    panels_ref,
    barrier_ref,
    counts_ref,
    diag_ref,
    cross_ref,
    rows,
    diagonal_row,
    count,
    weight_row,
    weight_peer,
    weight_col,
    right_t,
    left_t,
    total,
    out_tiles,
    in_tiles,
    peer_tiles,
    local_sem,
    peer_send,
    peer_recv,
    link_send,
    link_recv,
    pass_send,
    pass_recv,
):
    R = panels_ref.shape[1]
    B = panels_ref.shape[2] // 2
    H = B // 2
    Q = H // 2
    s, t, p = lax.axis_index("scen"), lax.axis_index("tm"), lax.axis_index("panel")
    q = 1 - p
    peer = (s, t, q)
    after = (s, lax.rem(t + 1, blocks), p)
    before = (s, lax.rem(t + blocks - 1, blocks), p)
    has_before, has_after = t > 0, t < blocks - 1

    local_right = pltpu.make_async_copy(
        panels_ref.at[0, :, pl.ds(B, B)], rows.at[pl.ds(0, R), pl.ds(B, B)], local_sem.at[0]
    )
    local_left = pltpu.make_async_copy(
        panels_ref.at[0, :, pl.ds(0, B)], rows.at[pl.ds(0, R), pl.ds(0, B)], local_sem.at[1]
    )
    diagonal_copy = pltpu.make_async_copy(barrier_ref, diagonal_row, local_sem.at[2])
    count_copy = pltpu.make_async_copy(counts_ref, count, local_sem.at[3])
    count_copy.start()
    diagonal_copy.start()
    local_right.start()
    local_left.start()

    entry = pltpu.get_barrier_semaphore()
    pl.semaphore_signal(entry, inc=1, device_id=peer, device_id_type=MESH)

    @pl.when(has_before)
    def _():
        pl.semaphore_signal(entry, inc=1, device_id=before, device_id_type=MESH)

    @pl.when(has_after)
    def _():
        pl.semaphore_signal(entry, inc=1, device_id=after, device_id_type=MESH)

    spot = lax.broadcasted_iota(jnp.int32, (8, R), 1)
    count_copy.wait()
    diagonal_copy.wait()
    diagonal = jnp.broadcast_to(diagonal_row[...].astype(F32), (8, R))
    weight_row[...] = jnp.where(spot < count[0, 0] * PR, diagonal, 0.0)

    def right_tile(half, tile):
        return pl.ds(pl.multiple_of(B + half * H + tile * Q, Q), Q)

    def to_peer(columns, which):
        return pltpu.make_async_remote_copy(
            src_ref=panels_ref.at[0, :, columns],
            dst_ref=rows.at[pl.ds(R, R), columns],
            send_sem=peer_send.at[which],
            recv_sem=peer_recv.at[which],
            device_id=peer,
            device_id_type=MESH,
        )

    def exchange(dest):
        rest = 1 - dest
        return [
            to_peer(right_tile(dest, 0), 0),
            to_peer(right_tile(rest, dest), 1),
            to_peer(right_tile(dest, 1), 2),
            to_peer(right_tile(rest, 1 - dest), 3),
            to_peer(pl.ds(pl.multiple_of(dest * H, H), H), 4),
            to_peer(pl.ds(pl.multiple_of(rest * H, H), H), 5),
        ]

    weight_copy = pltpu.make_async_remote_copy(
        src_ref=weight_row,
        dst_ref=weight_peer,
        send_sem=peer_send.at[6],
        recv_sem=peer_recv.at[6],
        device_id=peer,
        device_id_type=MESH,
    )
    pl.semaphore_wait(entry, 1 + has_before.astype(jnp.int32) + has_after.astype(jnp.int32))
    weight_copy.start()
    sent = exchange(q)
    came = exchange(p)
    for copy in sent:
        copy.start()

    def spread(row):
        return jnp.broadcast_to(row[0:1, :], (128, R)).T

    def scaled_t(group, columns, width):
        weight = weight_col[pl.ds(group * R, R), :]
        plain = rows[pl.ds(group * R, R), columns].astype(F32)
        weight = jnp.concatenate([weight] * (width // 128), axis=1)
        return (plain * weight).astype(BF16).T

    weight_col[pl.ds(0, R), :] = spread(weight_row[...])
    local_right.wait()
    for tile in range(2):
        right_t[pl.ds(tile * Q, Q), pl.ds(0, R)] = scaled_t(0, right_tile(p, tile), Q)
    weight_copy.wait_recv()
    weight_col[pl.ds(R, R), :] = spread(weight_peer[...])

    def link(first, length, which):
        return pltpu.make_async_remote_copy(
            src_ref=out_tiles.at[pl.ds(first, length), :],
            dst_ref=in_tiles.at[pl.ds(first, length), :],
            send_sem=link_send.at[which],
            recv_sem=link_recv.at[which],
            device_id=after,
            device_id_type=MESH,
        )

    links = [link(0, Q, 0), link(Q, Q, 1), link(2 * Q, Q, 2), link(3 * Q, Q + PAD, 3)]

    def send_on(which):
        @pl.when(has_after)
        def _():
            links[which].start()

    lower = lax.broadcasted_iota(jnp.int32, (Q, Q), 0)
    upper = lax.broadcasted_iota(jnp.int32, (Q, Q), 1)

    for tile in range(2):
        came[2 * tile].wait_recv()
        right_t[pl.ds(tile * Q, Q), pl.ds(R, R)] = scaled_t(1, right_tile(p, tile), Q)
        came[2 * tile + 1].wait_recv()
        other = lax.rem(tile + p, 2)
        out_tiles[pl.ds(tile * Q, Q), :] = gram(
            right_t[pl.ds(tile * Q, Q), :], rows[:, right_tile(q, other)]
        ).astype(BF16)
        send_on(tile)
    out_tiles[pl.ds(2 * Q, Q), :] = gram(
        right_t[pl.ds(0, Q), :], rows[:, right_tile(p, 1)]
    ).astype(BF16)
    send_on(2)
    first = gram(right_t[pl.ds(0, Q), :], rows[:, right_tile(p, 0)])
    second = gram(right_t[pl.ds(Q, Q), :], rows[:, right_tile(p, 1)])
    out_tiles[pl.ds(3 * Q, Q), :] = jnp.where(upper >= lower, first, second).astype(BF16)
    middle = jnp.sum(jnp.where(upper == lower, second, 0.0), axis=0, keepdims=True)
    out_tiles[pl.ds(4 * Q, PAD), :] = jnp.broadcast_to(middle, (PAD, Q)).astype(BF16)
    send_on(3)

    own_left = pl.ds(pl.multiple_of(p * H, H), H)
    local_left.wait()
    left_t[:, pl.ds(0, R)] = scaled_t(0, own_left, H)
    came[4].wait_recv()
    left_t[:, pl.ds(R, R)] = scaled_t(1, own_left, H)
    came[5].wait_recv()

    def left_step(step, carry):
        here = pl.ds(pl.multiple_of(step * Q, Q), Q)
        total[:, here] = gram(left_t[...], rows[:, here])
        return carry

    lax.fori_loop(0, B // Q, left_step, 0)

    def cross_step(step, carry):
        here = pl.ds(pl.multiple_of(step * Q, Q), Q)
        there = pl.ds(pl.multiple_of(B + step * Q, Q), Q)
        cross_ref[:, here] = gram(left_t[...], rows[:, there]).astype(BF16)
        return carry

    def handed(which):
        return pltpu.make_async_remote_copy(
            src_ref=in_tiles.at[pl.ds(which * Q, Q), :],
            dst_ref=peer_tiles.at[pl.ds(which * Q, Q), :],
            send_sem=pass_send.at[which],
            recv_sem=pass_recv.at[which],
            device_id=peer,
            device_id_type=MESH,
        )

    passes = [handed(0), handed(1)]

    @pl.when(has_before)
    def _():
        links[0].wait_recv()
        passes[0].start()

    lax.fori_loop(0, B // Q, cross_step, 0)

    def columns(half, tile):
        return pl.ds(pl.multiple_of(half * H + tile * Q, Q), Q)

    def band(tile):
        return pl.ds(pl.multiple_of(tile * Q, Q), Q)

    def put(row_tile, where, value):
        diag_ref[band(row_tile), where] = (total[band(row_tile), where] + value).astype(BF16)

    @pl.when(t == 0)
    def _():
        diag_ref[...] = total[...].astype(BF16)

    @pl.when(has_before)
    def _():
        put(0, columns(q, p), in_tiles[pl.ds(0, Q), :].astype(F32))
        links[1].wait_recv()
        passes[1].start()
        put(1, columns(q, 1 - p), in_tiles[pl.ds(Q, Q), :].astype(F32))
        for tile in range(2):
            passes[tile].wait_recv()
            turned = peer_tiles[pl.ds(tile * Q, Q), :].astype(F32).T
            put(lax.rem(tile + q, 2), columns(q, tile), turned)
        links[2].wait_recv()
        square = in_tiles[pl.ds(2 * Q, Q), :].astype(F32)
        put(0, columns(p, 1), square)
        put(1, columns(p, 0), square.T)
        links[3].wait_recv()
        packed = in_tiles[pl.ds(3 * Q, Q), :].astype(F32)
        turned = packed.T
        put(0, columns(p, 0), jnp.where(upper >= lower, packed, turned))
        middle_row = in_tiles[pl.ds(4 * Q, PAD), :].astype(F32)[0:1, :]
        put(
            1,
            columns(p, 1),
            jnp.where(
                upper == lower,
                jnp.broadcast_to(middle_row, (Q, Q)),
                jnp.where(upper < lower, packed, turned),
            ),
        )
        for copy in passes:
            copy.wait_send()

    weight_copy.wait_send()
    for copy in sent:
        copy.wait_send()

    @pl.when(has_after)
    def _():
        for copy in links:
            copy.wait_send()


def write_out(diag_ref, cross_ref, diag_out, cross_out, sems):
    length = diag_ref.shape[0] // PIECES
    copies = []
    for piece in range(PIECES):
        here = pl.ds(piece * length, length)
        copies.append(
            pltpu.make_async_copy(diag_ref.at[here], diag_out.at[0, here], sems.at[2 * piece])
        )
        copies.append(
            pltpu.make_async_copy(
                cross_ref.at[here], cross_out.at[0, here], sems.at[2 * piece + 1]
            )
        )
    for copy in copies:
        copy.start()
    for copy in copies:
        copy.wait()


def body(panels, barrier, counts):
    R = panels.shape[1]
    B = panels.shape[2] // 2
    H = B // 2
    Q = H // 2
    tiles = 4 * Q + PAD
    flops = 2 * 3 * H * B * 2 * R
    diag, cross = pl.pallas_call(
        functools.partial(kernel, lax.axis_size("tm")),
        out_shape=(
            jax.ShapeDtypeStruct((H, B), BF16),
            jax.ShapeDtypeStruct((H, B), BF16),
        ),
        in_specs=[
            pl.BlockSpec(memory_space=pltpu.HBM),
            pl.BlockSpec(memory_space=pltpu.HBM),
            pl.BlockSpec(memory_space=pltpu.HBM),
        ],
        out_specs=(
            pl.BlockSpec(memory_space=pltpu.VMEM),
            pl.BlockSpec(memory_space=pltpu.VMEM),
        ),
        scratch_shapes=[
            pltpu.VMEM((2 * R, 2 * B), BF16),
            pltpu.VMEM((1, R), BF16),
            pltpu.SMEM((1, 1), jnp.int32),
            pltpu.VMEM((8, R), F32),
            pltpu.VMEM((8, R), F32),
            pltpu.VMEM((2 * R, 128), F32),
            pltpu.VMEM((H, 2 * R), BF16),
            pltpu.VMEM((H, 2 * R), BF16),
            pltpu.VMEM((H, B), F32),
            pltpu.VMEM((tiles, Q), BF16),
            pltpu.VMEM((tiles, Q), BF16),
            pltpu.VMEM((2 * Q, Q), BF16),
            pltpu.SemaphoreType.DMA((4,)),
            pltpu.SemaphoreType.DMA((7,)),
            pltpu.SemaphoreType.DMA((7,)),
            pltpu.SemaphoreType.DMA((4,)),
            pltpu.SemaphoreType.DMA((4,)),
            pltpu.SemaphoreType.DMA((2,)),
            pltpu.SemaphoreType.DMA((2,)),
        ],
        compiler_params=pltpu.CompilerParams(
            collective_id=0, has_side_effects=True, vmem_limit_bytes=VMEM_BYTES
        ),
        cost_estimate=pl.CostEstimate(
            flops=flops, bytes_accessed=4 * R * B * 2 + 4 * H * B, transcendentals=0
        ),
    )(panels, barrier, counts)
    return tuple(
        pl.pallas_call(
            write_out,
            out_shape=(
                jax.ShapeDtypeStruct((1, H, B), BF16),
                jax.ShapeDtypeStruct((1, H, B), BF16),
            ),
            in_specs=[pl.BlockSpec(memory_space=pltpu.VMEM)] * 2,
            out_specs=(pl.BlockSpec(memory_space=pl.ANY), pl.BlockSpec(memory_space=pl.ANY)),
            scratch_shapes=[pltpu.SemaphoreType.DMA((2 * PIECES,))],
        )(diag, cross)
    )


def solution(mesh):
    return jax.shard_map(
        body,
        mesh=mesh,
        in_specs=(
            P(("scen", "tm"), "panel", None),
            P(("scen", "tm"), "panel"),
            P(("scen", "tm"), "panel"),
        ),
        out_specs=(P(("scen", "tm"), "panel", None), P(("scen", "tm"), "panel", None)),
        check_vma=False,
    )
```

```python
import functools

import jax
import jax.numpy as jnp
from jax import lax
from jax.experimental import pallas as pl
from jax.experimental.pallas import tpu as pltpu
from jax.sharding import PartitionSpec as P

PR = 64
VMEM_BYTES = 48 * 1024 * 1024
MESH = pl.DeviceIdType.MESH
F32 = jnp.float32
BF16 = jnp.bfloat16
PAD = 16


def gram(left, right):
    return jnp.dot(left, right, preferred_element_type=F32)


def kernel(
    blocks,
    panels_ref,
    barrier_ref,
    counts_ref,
    diag_ref,
    cross_ref,
    rows,
    diagonal_row,
    weight_row,
    weight_peer,
    weight_col,
    right_t,
    left_t,
    total,
    out_tiles,
    in_tiles,
    peer_tiles,
    local_sem,
    peer_send,
    peer_recv,
    link_send,
    link_recv,
    pass_send,
    pass_recv,
):
    R = panels_ref.shape[1]
    B = panels_ref.shape[2] // 2
    H = B // 2
    Q = H // 2
    E = Q // 2
    s, t, p = lax.axis_index("scen"), lax.axis_index("tm"), lax.axis_index("panel")
    q = 1 - p
    peer = (s, t, q)
    after = (s, lax.rem(t + 1, blocks), p)
    before = (s, lax.rem(t + blocks - 1, blocks), p)
    has_before, has_after = t > 0, t < blocks - 1

    local_right = pltpu.make_async_copy(
        panels_ref.at[0, :, pl.ds(B, B)], rows.at[pl.ds(0, R), pl.ds(B, B)], local_sem.at[0]
    )
    local_left = pltpu.make_async_copy(
        panels_ref.at[0, :, pl.ds(0, B)], rows.at[pl.ds(0, R), pl.ds(0, B)], local_sem.at[1]
    )
    diagonal_copy = pltpu.make_async_copy(barrier_ref, diagonal_row, local_sem.at[2])
    diagonal_copy.start()
    local_right.start()
    local_left.start()

    entry = pltpu.get_barrier_semaphore()
    pl.semaphore_signal(entry, inc=1, device_id=peer, device_id_type=MESH)

    @pl.when(has_before)
    def _():
        pl.semaphore_signal(entry, inc=1, device_id=before, device_id_type=MESH)

    @pl.when(has_after)
    def _():
        pl.semaphore_signal(entry, inc=1, device_id=after, device_id_type=MESH)

    spot = lax.broadcasted_iota(jnp.int32, (8, R), 1)
    diagonal_copy.wait()
    diagonal = jnp.broadcast_to(diagonal_row[...].astype(F32), (8, R))
    weight_row[...] = jnp.where(spot < counts_ref[0, 0] * PR, diagonal, 0.0)

    def right_tile(half, tile):
        return pl.ds(pl.multiple_of(B + half * H + tile * Q, Q), Q)

    def to_peer(columns, which):
        return pltpu.make_async_remote_copy(
            src_ref=panels_ref.at[0, :, columns],
            dst_ref=rows.at[pl.ds(R, R), columns],
            send_sem=peer_send.at[which],
            recv_sem=peer_recv.at[which],
            device_id=peer,
            device_id_type=MESH,
        )

    def exchange(dest):
        rest = 1 - dest
        return [
            to_peer(right_tile(dest, 0), 0),
            to_peer(right_tile(rest, dest), 1),
            to_peer(right_tile(dest, 1), 2),
            to_peer(right_tile(rest, 1 - dest), 3),
            to_peer(pl.ds(pl.multiple_of(dest * H, H), H), 4),
            to_peer(pl.ds(pl.multiple_of(rest * H, H), H), 5),
        ]

    weight_copy = pltpu.make_async_remote_copy(
        src_ref=weight_row,
        dst_ref=weight_peer,
        send_sem=peer_send.at[6],
        recv_sem=peer_recv.at[6],
        device_id=peer,
        device_id_type=MESH,
    )
    pl.semaphore_wait(entry, 1 + has_before.astype(jnp.int32) + has_after.astype(jnp.int32))
    weight_copy.start()
    sent = exchange(q)
    came = exchange(p)
    for copy in sent:
        copy.start()

    def spread(row):
        return jnp.broadcast_to(row[0:1, :], (128, R)).T

    def scaled_t(group, columns, width):
        weight = weight_col[pl.ds(group * R, R), :]
        plain = rows[pl.ds(group * R, R), columns].astype(F32)
        weight = jnp.concatenate([weight] * (width // 128), axis=1)
        return (plain * weight).astype(BF16).T

    weight_col[pl.ds(0, R), :] = spread(weight_row[...])
    local_right.wait()
    for tile in range(2):
        right_t[pl.ds(tile * Q, Q), pl.ds(0, R)] = scaled_t(0, right_tile(p, tile), Q)
    weight_copy.wait_recv()
    weight_col[pl.ds(R, R), :] = spread(weight_peer[...])

    def link(first, length, which):
        return pltpu.make_async_remote_copy(
            src_ref=out_tiles.at[pl.ds(first, length), :],
            dst_ref=in_tiles.at[pl.ds(first, length), :],
            send_sem=link_send.at[which],
            recv_sem=link_recv.at[which],
            device_id=after,
            device_id_type=MESH,
        )

    links = [
        link(0, Q, 0),
        link(Q, Q, 1),
        link(2 * Q, Q + PAD, 2),
        link(3 * Q + PAD, E, 3),
        link(3 * Q + PAD + E, E, 4),
    ]

    def send_on(which):
        @pl.when(has_after)
        def _():
            links[which].start()

    lower = lax.broadcasted_iota(jnp.int32, (Q, Q), 0)
    upper = lax.broadcasted_iota(jnp.int32, (Q, Q), 1)

    for tile in range(2):
        came[2 * tile].wait_recv()
        right_t[pl.ds(tile * Q, Q), pl.ds(R, R)] = scaled_t(1, right_tile(p, tile), Q)
        came[2 * tile + 1].wait_recv()
        other = lax.rem(tile + p, 2)
        out_tiles[pl.ds(tile * Q, Q), :] = gram(
            right_t[pl.ds(tile * Q, Q), :], rows[:, right_tile(q, other)]
        ).astype(BF16)
        send_on(tile)
    first = gram(right_t[pl.ds(0, Q), :], rows[:, right_tile(p, 0)])
    second = gram(right_t[pl.ds(Q, Q), :], rows[:, right_tile(p, 1)])
    out_tiles[pl.ds(2 * Q, Q), :] = jnp.where(upper >= lower, first, second).astype(BF16)
    middle = jnp.sum(jnp.where(upper == lower, second, 0.0), axis=0, keepdims=True)
    out_tiles[pl.ds(3 * Q, PAD), :] = jnp.broadcast_to(middle, (PAD, Q)).astype(BF16)
    send_on(2)
    for part in range(2):
        out_tiles[pl.ds(3 * Q + PAD + part * E, E), :] = gram(
            right_t[pl.ds(part * E, E), :], rows[:, right_tile(p, 1)]
        ).astype(BF16)
        send_on(3 + part)

    own_left = pl.ds(pl.multiple_of(p * H, H), H)
    local_left.wait()
    left_t[:, pl.ds(0, R)] = scaled_t(0, own_left, H)
    came[4].wait_recv()
    left_t[:, pl.ds(R, R)] = scaled_t(1, own_left, H)
    came[5].wait_recv()

    def left_step(step, carry):
        here = pl.ds(pl.multiple_of(step * Q, Q), Q)
        total[:, here] = gram(left_t[...], rows[:, here])
        return carry

    lax.fori_loop(0, B // Q, left_step, 0)

    def cross_step(step, carry):
        here = pl.ds(pl.multiple_of(step * Q, Q), Q)
        there = pl.ds(pl.multiple_of(B + step * Q, Q), Q)
        cross_ref[:, here] = gram(left_t[...], rows[:, there]).astype(BF16)
        return carry

    def handed(which):
        return pltpu.make_async_remote_copy(
            src_ref=in_tiles.at[pl.ds(which * Q, Q), :],
            dst_ref=peer_tiles.at[pl.ds(which * Q, Q), :],
            send_sem=pass_send.at[which],
            recv_sem=pass_recv.at[which],
            device_id=peer,
            device_id_type=MESH,
        )

    passes = [handed(0), handed(1)]

    @pl.when(has_before)
    def _():
        links[0].wait_recv()
        passes[0].start()

    lax.fori_loop(0, B // Q, cross_step, 0)

    def columns(half, tile):
        return pl.ds(pl.multiple_of(half * H + tile * Q, Q), Q)

    def band(tile):
        return pl.ds(pl.multiple_of(tile * Q, Q), Q)

    def put(row_tile, where, value):
        diag_ref[band(row_tile), where] = (total[band(row_tile), where] + value).astype(BF16)

    @pl.when(t == 0)
    def _():
        diag_ref[...] = total[...].astype(BF16)

    @pl.when(has_before)
    def _():
        put(0, columns(q, p), in_tiles[pl.ds(0, Q), :].astype(F32))
        links[1].wait_recv()
        passes[1].start()
        put(1, columns(q, 1 - p), in_tiles[pl.ds(Q, Q), :].astype(F32))
        for tile in range(2):
            passes[tile].wait_recv()
            turned = peer_tiles[pl.ds(tile * Q, Q), :].astype(F32).T
            put(lax.rem(tile + q, 2), columns(q, tile), turned)
        links[2].wait_recv()
        packed = in_tiles[pl.ds(2 * Q, Q), :].astype(F32)
        turned = packed.T
        put(0, columns(p, 0), jnp.where(upper >= lower, packed, turned))
        middle_row = in_tiles[pl.ds(3 * Q, PAD), :].astype(F32)[0:1, :]
        put(
            1,
            columns(p, 1),
            jnp.where(
                upper == lower,
                jnp.broadcast_to(middle_row, (Q, Q)),
                jnp.where(upper < lower, packed, turned),
            ),
        )
        for part in range(2):
            links[3 + part].wait_recv()
            piece = in_tiles[pl.ds(3 * Q + PAD + part * E, E), :].astype(F32)
            across = pl.ds(part * E, E)
            diag_ref[across, columns(p, 1)] = (total[across, columns(p, 1)] + piece).astype(BF16)
            down = pl.ds(pl.multiple_of(p * H + part * E, E), E)
            diag_ref[pl.ds(Q, Q), down] = (total[pl.ds(Q, Q), down] + piece.T).astype(BF16)
        for copy in passes:
            copy.wait_send()

    weight_copy.wait_send()
    for copy in sent:
        copy.wait_send()

    @pl.when(has_after)
    def _():
        for copy in links:
            copy.wait_send()


def in_hbm(array):
    return pltpu.with_memory_space_constraint(array, pltpu.HBM)


def body(panels, barrier, counts):
    R = panels.shape[1]
    B = panels.shape[2] // 2
    H = B // 2
    Q = H // 2
    tiles = 4 * Q + PAD
    flops = 2 * 3 * H * B * 2 * R
    diag, cross = pl.pallas_call(
        functools.partial(kernel, lax.axis_size("tm")),
        out_shape=(
            jax.ShapeDtypeStruct((H, B), BF16),
            jax.ShapeDtypeStruct((H, B), BF16),
        ),
        in_specs=[
            pl.BlockSpec(memory_space=pltpu.HBM),
            pl.BlockSpec(memory_space=pltpu.HBM),
            pl.BlockSpec(memory_space=pltpu.SMEM),
        ],
        out_specs=(
            pl.BlockSpec(memory_space=pltpu.VMEM),
            pl.BlockSpec(memory_space=pltpu.VMEM),
        ),
        scratch_shapes=[
            pltpu.VMEM((2 * R, 2 * B), BF16),
            pltpu.VMEM((1, R), BF16),
            pltpu.VMEM((8, R), F32),
            pltpu.VMEM((8, R), F32),
            pltpu.VMEM((2 * R, 128), F32),
            pltpu.VMEM((H, 2 * R), BF16),
            pltpu.VMEM((H, 2 * R), BF16),
            pltpu.VMEM((H, B), F32),
            pltpu.VMEM((tiles, Q), BF16),
            pltpu.VMEM((tiles, Q), BF16),
            pltpu.VMEM((2 * Q, Q), BF16),
            pltpu.SemaphoreType.DMA((3,)),
            pltpu.SemaphoreType.DMA((7,)),
            pltpu.SemaphoreType.DMA((7,)),
            pltpu.SemaphoreType.DMA((5,)),
            pltpu.SemaphoreType.DMA((5,)),
            pltpu.SemaphoreType.DMA((2,)),
            pltpu.SemaphoreType.DMA((2,)),
        ],
        compiler_params=pltpu.CompilerParams(
            collective_id=0, has_side_effects=True, vmem_limit_bytes=VMEM_BYTES
        ),
        cost_estimate=pl.CostEstimate(
            flops=flops, bytes_accessed=4 * R * B * 2 + 4 * H * B, transcendentals=0
        ),
    )(in_hbm(panels), in_hbm(barrier), counts)
    return diag[None], cross[None]


def solution(mesh):
    return jax.shard_map(
        body,
        mesh=mesh,
        in_specs=(
            P(("scen", "tm"), "panel", None),
            P(("scen", "tm"), "panel"),
            P(("scen", "tm"), "panel"),
        ),
        out_specs=(P(("scen", "tm"), "panel", None), P(("scen", "tm"), "panel", None)),
        check_vma=False,
    )
```

```python
import functools

import jax
import jax.numpy as jnp
from jax import lax
from jax.experimental import pallas as pl
from jax.experimental.pallas import tpu as pltpu
from jax.sharding import PartitionSpec as P

PR = 64
VMEM_BYTES = 48 * 1024 * 1024
MESH = pl.DeviceIdType.MESH
F32 = jnp.float32
BF16 = jnp.bfloat16
PAD = 16


def gram(left, right):
    return jnp.dot(left, right, preferred_element_type=F32)


def kernel(
    blocks,
    panels_ref,
    barrier_ref,
    counts_ref,
    diag_ref,
    cross_ref,
    rows,
    diagonal_row,
    weight_row,
    weight_peer,
    weight_col,
    right_t,
    left_t,
    total,
    part_out,
    part_in,
    out_tiles,
    in_tiles,
    peer_tiles,
    local_sem,
    peer_send,
    peer_recv,
    part_send,
    part_recv,
    link_send,
    link_recv,
    pass_send,
    pass_recv,
):
    R = panels_ref.shape[1]
    B = panels_ref.shape[2] // 2
    H = B // 2
    Q = H // 2
    E = Q // 2
    s, t, p = lax.axis_index("scen"), lax.axis_index("tm"), lax.axis_index("panel")
    q = 1 - p
    peer = (s, t, q)
    after = (s, lax.rem(t + 1, blocks), p)
    before = (s, lax.rem(t + blocks - 1, blocks), p)
    has_before, has_after = t > 0, t < blocks - 1

    def right_tile(half, tile):
        return pl.ds(pl.multiple_of(B + half * H + tile * Q, Q), Q)

    def local(columns, which):
        return pltpu.make_async_copy(
            panels_ref.at[0, :, columns], rows.at[pl.ds(0, R), columns], local_sem.at[which]
        )

    diagonal_copy = pltpu.make_async_copy(barrier_ref, diagonal_row, local_sem.at[5])
    diagonal_copy.start()
    local_right = [
        local(right_tile(q, 0), 0),
        local(right_tile(p, q), 1),
        local(right_tile(q, 1), 2),
        local(right_tile(p, p), 3),
    ]
    local_left = local(pl.ds(0, B), 4)
    for copy in local_right:
        copy.start()
    local_left.start()

    entry = pltpu.get_barrier_semaphore()
    pl.semaphore_signal(entry, inc=1, device_id=peer, device_id_type=MESH)

    @pl.when(has_before)
    def _():
        pl.semaphore_signal(entry, inc=1, device_id=before, device_id_type=MESH)

    @pl.when(has_after)
    def _():
        pl.semaphore_signal(entry, inc=1, device_id=after, device_id_type=MESH)

    spot = lax.broadcasted_iota(jnp.int32, (8, R), 1)
    diagonal_copy.wait()
    diagonal = jnp.broadcast_to(diagonal_row[...].astype(F32), (8, R))
    weight_row[...] = jnp.where(spot < counts_ref[0, 0] * PR, diagonal, 0.0)

    def to_peer(columns, which):
        return pltpu.make_async_remote_copy(
            src_ref=panels_ref.at[0, :, columns],
            dst_ref=rows.at[pl.ds(R, R), columns],
            send_sem=peer_send.at[which],
            recv_sem=peer_recv.at[which],
            device_id=peer,
            device_id_type=MESH,
        )

    def exchange(dest):
        return [
            to_peer(pl.ds(pl.multiple_of(dest * H, H), H), 0),
            to_peer(pl.ds(pl.multiple_of((1 - dest) * H, H), H), 1),
            to_peer(pl.ds(B, H), 2),
            to_peer(pl.ds(B + H, H), 3),
        ]

    sent = exchange(q)
    came = exchange(p)

    weight_copy = pltpu.make_async_remote_copy(
        src_ref=weight_row,
        dst_ref=weight_peer,
        send_sem=peer_send.at[4],
        recv_sem=peer_recv.at[4],
        device_id=peer,
        device_id_type=MESH,
    )
    def spread(row):
        return jnp.broadcast_to(row[0:1, :], (128, R)).T

    def scaled_t(group, columns, width):
        weight = weight_col[pl.ds(group * R, R), :]
        plain = rows[pl.ds(group * R, R), columns].astype(F32)
        weight = jnp.concatenate([weight] * (width // 128), axis=1)
        return (plain * weight).astype(BF16).T

    def link(first, length, which):
        return pltpu.make_async_remote_copy(
            src_ref=out_tiles.at[pl.ds(first, length), :],
            dst_ref=in_tiles.at[pl.ds(first, length), :],
            send_sem=link_send.at[which],
            recv_sem=link_recv.at[which],
            device_id=after,
            device_id_type=MESH,
        )

    links = [
        link(0, Q, 0),
        link(Q, Q, 1),
        link(2 * Q, Q + PAD, 2),
        link(3 * Q + PAD, E, 3),
        link(3 * Q + PAD + E, E, 4),
    ]

    def send_on(which):
        @pl.when(has_after)
        def _():
            links[which].start()

    lower = lax.broadcasted_iota(jnp.int32, (Q, Q), 0)
    upper = lax.broadcasted_iota(jnp.int32, (Q, Q), 1)

    def part(first, length, which):
        return pltpu.make_async_remote_copy(
            src_ref=part_out.at[pl.ds(first, length), :],
            dst_ref=part_in.at[pl.ds(first, length), :],
            send_sem=part_send.at[which],
            recv_sem=part_recv.at[which],
            device_id=peer,
            device_id_type=MESH,
        )

    parts = [part(0, Q, 0), part(Q, Q, 1), part(2 * Q, Q + PAD, 2), part(3 * Q + PAD, Q, 3)]

    def turn(dest, tile):
        half = q if dest else p
        right_t[pl.ds((2 - 2 * dest + tile) * Q, Q), :] = scaled_t(0, right_tile(half, tile), Q)

    def side(dest, tile):
        return right_t[pl.ds((2 - 2 * dest + tile) * Q, Q), :]

    def own(columns):
        return rows[pl.ds(0, R), columns]

    def across_tile(dest, tile):
        home, away = (q, p) if dest else (p, q)
        return gram(side(dest, tile), own(right_tile(away, lax.rem(tile + home, 2))))

    def packed_tile(dest):
        home = q if dest else p
        first = gram(side(dest, 0), own(right_tile(home, 0)))
        second = gram(side(dest, 1), own(right_tile(home, 1)))
        middle = jnp.sum(jnp.where(upper == lower, second, 0.0), axis=0, keepdims=True)
        return jnp.where(upper >= lower, first, second), jnp.broadcast_to(middle, (PAD, Q))

    def square_tile(dest):
        home = q if dest else p
        return gram(side(dest, 0), own(right_tile(home, 1)))

    weight_col[pl.ds(0, R), :] = spread(weight_row[...])
    local_right[0].wait()
    turn(1, 0)
    local_right[1].wait()
    part_out[pl.ds(0, Q), :] = across_tile(1, 0).astype(BF16)
    pl.semaphore_wait(entry, 1 + has_before.astype(jnp.int32) + has_after.astype(jnp.int32))
    parts[0].start()
    weight_copy.start()
    local_right[2].wait()
    local_right[3].wait()
    turn(1, 1)
    part_out[pl.ds(Q, Q), :] = across_tile(1, 1).astype(BF16)
    parts[1].start()
    sent[0].start()
    sent[1].start()
    turn(0, 0)
    mine = across_tile(0, 0)
    parts[0].wait_recv()
    out_tiles[pl.ds(0, Q), :] = (mine + part_in[pl.ds(0, Q), :].astype(F32)).astype(BF16)
    send_on(0)

    packed, middle = packed_tile(1)
    part_out[pl.ds(2 * Q, Q), :] = packed.astype(BF16)
    part_out[pl.ds(3 * Q, PAD), :] = middle.astype(BF16)
    parts[2].start()
    part_out[pl.ds(3 * Q + PAD, Q), :] = square_tile(1).astype(BF16)
    parts[3].start()
    sent[2].start()
    sent[3].start()

    turn(0, 1)
    mine = across_tile(0, 1)
    parts[1].wait_recv()
    out_tiles[pl.ds(Q, Q), :] = (mine + part_in[pl.ds(Q, Q), :].astype(F32)).astype(BF16)
    send_on(1)

    packed, middle = packed_tile(0)
    parts[2].wait_recv()
    out_tiles[pl.ds(2 * Q, Q), :] = (
        packed + part_in[pl.ds(2 * Q, Q), :].astype(F32)
    ).astype(BF16)
    out_tiles[pl.ds(3 * Q, PAD), :] = (
        middle + part_in[pl.ds(3 * Q, PAD), :].astype(F32)
    ).astype(BF16)
    send_on(2)
    mine = square_tile(0)
    parts[3].wait_recv()
    out_tiles[pl.ds(3 * Q + PAD, Q), :] = (
        mine + part_in[pl.ds(3 * Q + PAD, Q), :].astype(F32)
    ).astype(BF16)
    send_on(3)
    send_on(4)

    weight_copy.wait_recv()
    weight_col[pl.ds(R, R), :] = spread(weight_peer[...])
    own_left = pl.ds(pl.multiple_of(p * H, H), H)
    local_left.wait()
    left_t[:, pl.ds(0, R)] = scaled_t(0, own_left, H)
    came[0].wait_recv()
    left_t[:, pl.ds(R, R)] = scaled_t(1, own_left, H)
    came[1].wait_recv()

    def left_step(step, carry):
        here = pl.ds(pl.multiple_of(step * Q, Q), Q)
        total[:, here] = gram(left_t[...], rows[:, here])
        return carry

    lax.fori_loop(0, B // Q, left_step, 0)

    def cross_step(step, carry):
        here = pl.ds(pl.multiple_of(step * Q, Q), Q)
        there = pl.ds(pl.multiple_of(B + step * Q, Q), Q)
        cross_ref[:, here] = gram(left_t[...], rows[:, there]).astype(BF16)
        return carry

    def handed(which):
        return pltpu.make_async_remote_copy(
            src_ref=in_tiles.at[pl.ds(which * Q, Q), :],
            dst_ref=peer_tiles.at[pl.ds(which * Q, Q), :],
            send_sem=pass_send.at[which],
            recv_sem=pass_recv.at[which],
            device_id=peer,
            device_id_type=MESH,
        )

    passes = [handed(0), handed(1)]

    @pl.when(has_before)
    def _():
        links[0].wait_recv()
        passes[0].start()

    came[2].wait_recv()
    came[3].wait_recv()
    lax.fori_loop(0, B // Q, cross_step, 0)

    def columns(half, tile):
        return pl.ds(pl.multiple_of(half * H + tile * Q, Q), Q)

    def band(tile):
        return pl.ds(pl.multiple_of(tile * Q, Q), Q)

    def put(row_tile, where, value):
        diag_ref[band(row_tile), where] = (total[band(row_tile), where] + value).astype(BF16)

    @pl.when(t == 0)
    def _():
        diag_ref[...] = total[...].astype(BF16)

    @pl.when(has_before)
    def _():
        put(0, columns(q, p), in_tiles[pl.ds(0, Q), :].astype(F32))
        links[1].wait_recv()
        passes[1].start()
        put(1, columns(q, 1 - p), in_tiles[pl.ds(Q, Q), :].astype(F32))
        for tile in range(2):
            passes[tile].wait_recv()
            turned = peer_tiles[pl.ds(tile * Q, Q), :].astype(F32).T
            put(lax.rem(tile + q, 2), columns(q, tile), turned)
        links[2].wait_recv()
        packed = in_tiles[pl.ds(2 * Q, Q), :].astype(F32)
        turned = packed.T
        put(0, columns(p, 0), jnp.where(upper >= lower, packed, turned))
        middle_row = in_tiles[pl.ds(3 * Q, PAD), :].astype(F32)[0:1, :]
        put(
            1,
            columns(p, 1),
            jnp.where(
                upper == lower,
                jnp.broadcast_to(middle_row, (Q, Q)),
                jnp.where(upper < lower, packed, turned),
            ),
        )
        for part in range(2):
            links[3 + part].wait_recv()
            piece = in_tiles[pl.ds(3 * Q + PAD + part * E, E), :].astype(F32)
            across = pl.ds(part * E, E)
            diag_ref[across, columns(p, 1)] = (total[across, columns(p, 1)] + piece).astype(BF16)
            down = pl.ds(pl.multiple_of(p * H + part * E, E), E)
            diag_ref[pl.ds(Q, Q), down] = (total[pl.ds(Q, Q), down] + piece.T).astype(BF16)
        for copy in passes:
            copy.wait_send()

    weight_copy.wait_send()
    for copy in sent + parts:
        copy.wait_send()

    @pl.when(has_after)
    def _():
        for copy in links:
            copy.wait_send()


def in_hbm(array):
    return pltpu.with_memory_space_constraint(array, pltpu.HBM)


def body(panels, barrier, counts):
    R = panels.shape[1]
    B = panels.shape[2] // 2
    H = B // 2
    Q = H // 2
    tiles = 4 * Q + PAD
    flops = 2 * 3 * H * B * 2 * R
    diag, cross = pl.pallas_call(
        functools.partial(kernel, lax.axis_size("tm")),
        out_shape=(
            jax.ShapeDtypeStruct((H, B), BF16),
            jax.ShapeDtypeStruct((H, B), BF16),
        ),
        in_specs=[
            pl.BlockSpec(memory_space=pltpu.HBM),
            pl.BlockSpec(memory_space=pltpu.HBM),
            pl.BlockSpec(memory_space=pltpu.SMEM),
        ],
        out_specs=(
            pl.BlockSpec(memory_space=pltpu.VMEM),
            pl.BlockSpec(memory_space=pltpu.VMEM),
        ),
        scratch_shapes=[
            pltpu.VMEM((2 * R, 2 * B), BF16),
            pltpu.VMEM((1, R), BF16),
            pltpu.VMEM((8, R), F32),
            pltpu.VMEM((8, R), F32),
            pltpu.VMEM((2 * R, 128), F32),
            pltpu.VMEM((B, R), BF16),
            pltpu.VMEM((H, 2 * R), BF16),
            pltpu.VMEM((H, B), F32),
            pltpu.VMEM((tiles, Q), BF16),
            pltpu.VMEM((tiles, Q), BF16),
            pltpu.VMEM((tiles, Q), BF16),
            pltpu.VMEM((tiles, Q), BF16),
            pltpu.VMEM((2 * Q, Q), BF16),
            pltpu.SemaphoreType.DMA((6,)),
            pltpu.SemaphoreType.DMA((5,)),
            pltpu.SemaphoreType.DMA((5,)),
            pltpu.SemaphoreType.DMA((4,)),
            pltpu.SemaphoreType.DMA((4,)),
            pltpu.SemaphoreType.DMA((5,)),
            pltpu.SemaphoreType.DMA((5,)),
            pltpu.SemaphoreType.DMA((2,)),
            pltpu.SemaphoreType.DMA((2,)),
        ],
        compiler_params=pltpu.CompilerParams(
            collective_id=0, has_side_effects=True, vmem_limit_bytes=VMEM_BYTES
        ),
        cost_estimate=pl.CostEstimate(
            flops=flops, bytes_accessed=4 * R * B * 2 + 4 * H * B, transcendentals=0
        ),
    )(in_hbm(panels), in_hbm(barrier), counts)
    return diag[None], cross[None]


def solution(mesh):
    return jax.shard_map(
        body,
        mesh=mesh,
        in_specs=(
            P(("scen", "tm"), "panel", None),
            P(("scen", "tm"), "panel"),
            P(("scen", "tm"), "panel"),
        ),
        out_specs=(P(("scen", "tm"), "panel", None), P(("scen", "tm"), "panel", None)),
        check_vma=False,
    )
```

```python
import functools

import jax
import jax.numpy as jnp
from jax import lax
from jax.experimental import pallas as pl
from jax.experimental.pallas import tpu as pltpu
from jax.sharding import PartitionSpec as P

PR = 64
VMEM_BYTES = 48 * 1024 * 1024
MESH = pl.DeviceIdType.MESH
F32 = jnp.float32
BF16 = jnp.bfloat16
PAD = 16


def gram(left, right):
    return jnp.dot(left, right, preferred_element_type=F32)


def kernel(
    blocks,
    panels_ref,
    barrier_ref,
    counts_ref,
    diag_ref,
    cross_ref,
    rows,
    diagonal_row,
    weight_row,
    weight_peer,
    weight_col,
    right_t,
    left_t,
    total,
    part_out,
    part_in,
    out_tiles,
    in_tiles,
    peer_tiles,
    local_sem,
    peer_send,
    peer_recv,
    part_send,
    part_recv,
    link_send,
    link_recv,
    pass_send,
    pass_recv,
):
    R = panels_ref.shape[1]
    B = panels_ref.shape[2] // 2
    H = B // 2
    Q = H // 2
    E = Q // 2
    s, t, p = lax.axis_index("scen"), lax.axis_index("tm"), lax.axis_index("panel")
    q = 1 - p
    peer = (s, t, q)
    after = (s, lax.rem(t + 1, blocks), p)
    before = (s, lax.rem(t + blocks - 1, blocks), p)
    has_before, has_after = t > 0, t < blocks - 1

    def right_tile(half, tile):
        return pl.ds(pl.multiple_of(B + half * H + tile * Q, Q), Q)

    def local(columns, which):
        return pltpu.make_async_copy(
            panels_ref.at[0, :, columns], rows.at[pl.ds(0, R), columns], local_sem.at[which]
        )

    diagonal_copy = pltpu.make_async_copy(barrier_ref, diagonal_row, local_sem.at[5])
    diagonal_copy.start()
    local_right = [
        local(right_tile(q, 0), 0),
        local(right_tile(p, q), 1),
        local(right_tile(q, 1), 2),
        local(right_tile(p, p), 3),
    ]
    local_left = local(pl.ds(0, B), 4)
    for copy in local_right:
        copy.start()
    local_left.start()

    entry = pltpu.get_barrier_semaphore()
    pl.semaphore_signal(entry, inc=1, device_id=peer, device_id_type=MESH)

    @pl.when(has_before)
    def _():
        pl.semaphore_signal(entry, inc=1, device_id=before, device_id_type=MESH)

    @pl.when(has_after)
    def _():
        pl.semaphore_signal(entry, inc=1, device_id=after, device_id_type=MESH)

    spot = lax.broadcasted_iota(jnp.int32, (8, R), 1)
    diagonal_copy.wait()
    diagonal = jnp.broadcast_to(diagonal_row[...].astype(F32), (8, R))
    weight_row[...] = jnp.where(spot < counts_ref[0, 0] * PR, diagonal, 0.0)

    def to_peer(columns, which):
        return pltpu.make_async_remote_copy(
            src_ref=panels_ref.at[0, :, columns],
            dst_ref=rows.at[pl.ds(R, R), columns],
            send_sem=peer_send.at[which],
            recv_sem=peer_recv.at[which],
            device_id=peer,
            device_id_type=MESH,
        )

    def exchange(dest):
        return [
            to_peer(pl.ds(pl.multiple_of(dest * H, H), H), 0),
            to_peer(pl.ds(pl.multiple_of((1 - dest) * H, H), H), 1),
            to_peer(pl.ds(B, H), 2),
            to_peer(pl.ds(B + H, H), 3),
        ]

    sent = exchange(q)
    came = exchange(p)

    weight_copy = pltpu.make_async_remote_copy(
        src_ref=weight_row,
        dst_ref=weight_peer,
        send_sem=peer_send.at[4],
        recv_sem=peer_recv.at[4],
        device_id=peer,
        device_id_type=MESH,
    )
    def spread(row):
        return jnp.broadcast_to(row[0:1, :], (128, R)).T

    def scaled_t(group, columns, width):
        weight = weight_col[pl.ds(group * R, R), :]
        plain = rows[pl.ds(group * R, R), columns].astype(F32)
        weight = jnp.concatenate([weight] * (width // 128), axis=1)
        return (plain * weight).astype(BF16).T

    def link(first, length, which):
        return pltpu.make_async_remote_copy(
            src_ref=out_tiles.at[pl.ds(first, length), :],
            dst_ref=in_tiles.at[pl.ds(first, length), :],
            send_sem=link_send.at[which],
            recv_sem=link_recv.at[which],
            device_id=after,
            device_id_type=MESH,
        )

    links = [
        link(0, E, 0),
        link(Q, Q, 1),
        link(2 * Q, Q + PAD, 2),
        link(3 * Q + PAD, E, 3),
        link(3 * Q + PAD + E, E, 4),
        link(E, E, 5),
    ]

    def send_on(which):
        @pl.when(has_after)
        def _():
            links[which].start()

    lower = lax.broadcasted_iota(jnp.int32, (Q, Q), 0)
    upper = lax.broadcasted_iota(jnp.int32, (Q, Q), 1)

    def part(first, length, which):
        return pltpu.make_async_remote_copy(
            src_ref=part_out.at[pl.ds(first, length), :],
            dst_ref=part_in.at[pl.ds(first, length), :],
            send_sem=part_send.at[which],
            recv_sem=part_recv.at[which],
            device_id=peer,
            device_id_type=MESH,
        )

    parts = [
        part(0, E, 0),
        part(Q, Q, 1),
        part(2 * Q, Q + PAD, 2),
        part(3 * Q + PAD, Q, 3),
        part(E, E, 4),
    ]

    def turn(dest, tile):
        half = q if dest else p
        right_t[pl.ds((2 - 2 * dest + tile) * Q, Q), :] = scaled_t(0, right_tile(half, tile), Q)

    def side(dest, tile):
        return right_t[pl.ds((2 - 2 * dest + tile) * Q, Q), :]

    def own(columns):
        return rows[pl.ds(0, R), columns]

    def across_tile(dest, tile):
        home, away = (q, p) if dest else (p, q)
        return gram(side(dest, tile), own(right_tile(away, lax.rem(tile + home, 2))))

    def packed_tile(dest):
        home = q if dest else p
        first = gram(side(dest, 0), own(right_tile(home, 0)))
        second = gram(side(dest, 1), own(right_tile(home, 1)))
        middle = jnp.sum(jnp.where(upper == lower, second, 0.0), axis=0, keepdims=True)
        return jnp.where(upper >= lower, first, second), jnp.broadcast_to(middle, (PAD, Q))

    def square_tile(dest):
        home = q if dest else p
        return gram(side(dest, 0), own(right_tile(home, 1)))

    weight_col[pl.ds(0, R), :] = spread(weight_row[...])
    local_right[0].wait()
    turn(1, 0)
    local_right[1].wait()
    part_out[pl.ds(0, Q), :] = across_tile(1, 0).astype(BF16)
    pl.semaphore_wait(entry, 1 + has_before.astype(jnp.int32) + has_after.astype(jnp.int32))
    parts[0].start()
    parts[4].start()
    local_right[2].wait()
    local_right[3].wait()
    turn(0, 0)
    mine = across_tile(0, 0)
    parts[0].wait_recv()
    out_tiles[pl.ds(0, E), :] = (mine[:E] + part_in[pl.ds(0, E), :].astype(F32)).astype(BF16)
    send_on(0)
    parts[4].wait_recv()
    out_tiles[pl.ds(E, E), :] = (mine[E:] + part_in[pl.ds(E, E), :].astype(F32)).astype(BF16)
    send_on(5)

    turn(1, 1)
    part_out[pl.ds(Q, Q), :] = across_tile(1, 1).astype(BF16)
    parts[1].start()
    weight_copy.start()
    sent[0].start()
    sent[1].start()
    packed, middle = packed_tile(1)
    part_out[pl.ds(2 * Q, Q), :] = packed.astype(BF16)
    part_out[pl.ds(3 * Q, PAD), :] = middle.astype(BF16)
    parts[2].start()
    part_out[pl.ds(3 * Q + PAD, Q), :] = square_tile(1).astype(BF16)
    parts[3].start()
    sent[2].start()
    sent[3].start()

    turn(0, 1)
    mine = across_tile(0, 1)
    parts[1].wait_recv()
    out_tiles[pl.ds(Q, Q), :] = (mine + part_in[pl.ds(Q, Q), :].astype(F32)).astype(BF16)
    send_on(1)

    packed, middle = packed_tile(0)
    parts[2].wait_recv()
    out_tiles[pl.ds(2 * Q, Q), :] = (
        packed + part_in[pl.ds(2 * Q, Q), :].astype(F32)
    ).astype(BF16)
    out_tiles[pl.ds(3 * Q, PAD), :] = (
        middle + part_in[pl.ds(3 * Q, PAD), :].astype(F32)
    ).astype(BF16)
    send_on(2)
    mine = square_tile(0)
    parts[3].wait_recv()
    out_tiles[pl.ds(3 * Q + PAD, Q), :] = (
        mine + part_in[pl.ds(3 * Q + PAD, Q), :].astype(F32)
    ).astype(BF16)
    send_on(3)
    send_on(4)

    weight_copy.wait_recv()
    weight_col[pl.ds(R, R), :] = spread(weight_peer[...])
    own_left = pl.ds(pl.multiple_of(p * H, H), H)
    local_left.wait()
    left_t[:, pl.ds(0, R)] = scaled_t(0, own_left, H)
    came[0].wait_recv()
    left_t[:, pl.ds(R, R)] = scaled_t(1, own_left, H)
    came[1].wait_recv()

    def left_step(step, carry):
        here = pl.ds(pl.multiple_of(step * Q, Q), Q)
        total[:, here] = gram(left_t[...], rows[:, here])
        return carry

    lax.fori_loop(0, B // Q, left_step, 0)

    def cross_step(step, carry):
        here = pl.ds(pl.multiple_of(step * Q, Q), Q)
        there = pl.ds(pl.multiple_of(B + step * Q, Q), Q)
        cross_ref[:, here] = gram(left_t[...], rows[:, there]).astype(BF16)
        return carry

    def handed(which):
        return pltpu.make_async_remote_copy(
            src_ref=in_tiles.at[pl.ds(which * Q, Q), :],
            dst_ref=peer_tiles.at[pl.ds(which * Q, Q), :],
            send_sem=pass_send.at[which],
            recv_sem=pass_recv.at[which],
            device_id=peer,
            device_id_type=MESH,
        )

    passes = [handed(0), handed(1)]

    @pl.when(has_before)
    def _():
        links[0].wait_recv()
        links[5].wait_recv()
        passes[0].start()

    came[2].wait_recv()
    came[3].wait_recv()
    lax.fori_loop(0, B // Q, cross_step, 0)

    def columns(half, tile):
        return pl.ds(pl.multiple_of(half * H + tile * Q, Q), Q)

    def band(tile):
        return pl.ds(pl.multiple_of(tile * Q, Q), Q)

    def put(row_tile, where, value):
        diag_ref[band(row_tile), where] = (total[band(row_tile), where] + value).astype(BF16)

    @pl.when(t == 0)
    def _():
        diag_ref[...] = total[...].astype(BF16)

    @pl.when(has_before)
    def _():
        put(0, columns(q, p), in_tiles[pl.ds(0, Q), :].astype(F32))
        links[1].wait_recv()
        passes[1].start()
        put(1, columns(q, 1 - p), in_tiles[pl.ds(Q, Q), :].astype(F32))
        for tile in range(2):
            passes[tile].wait_recv()
            turned = peer_tiles[pl.ds(tile * Q, Q), :].astype(F32).T
            put(lax.rem(tile + q, 2), columns(q, tile), turned)
        links[2].wait_recv()
        packed = in_tiles[pl.ds(2 * Q, Q), :].astype(F32)
        turned = packed.T
        put(0, columns(p, 0), jnp.where(upper >= lower, packed, turned))
        middle_row = in_tiles[pl.ds(3 * Q, PAD), :].astype(F32)[0:1, :]
        put(
            1,
            columns(p, 1),
            jnp.where(
                upper == lower,
                jnp.broadcast_to(middle_row, (Q, Q)),
                jnp.where(upper < lower, packed, turned),
            ),
        )
        for part in range(2):
            links[3 + part].wait_recv()
            piece = in_tiles[pl.ds(3 * Q + PAD + part * E, E), :].astype(F32)
            across = pl.ds(part * E, E)
            diag_ref[across, columns(p, 1)] = (total[across, columns(p, 1)] + piece).astype(BF16)
            down = pl.ds(pl.multiple_of(p * H + part * E, E), E)
            diag_ref[pl.ds(Q, Q), down] = (total[pl.ds(Q, Q), down] + piece.T).astype(BF16)
        for copy in passes:
            copy.wait_send()

    weight_copy.wait_send()
    for copy in sent + parts:
        copy.wait_send()

    @pl.when(has_after)
    def _():
        for copy in links:
            copy.wait_send()


def in_hbm(array):
    return pltpu.with_memory_space_constraint(array, pltpu.HBM)


def body(panels, barrier, counts):
    R = panels.shape[1]
    B = panels.shape[2] // 2
    H = B // 2
    Q = H // 2
    tiles = 4 * Q + PAD
    flops = 2 * 3 * H * B * 2 * R
    diag, cross = pl.pallas_call(
        functools.partial(kernel, lax.axis_size("tm")),
        out_shape=(
            jax.ShapeDtypeStruct((H, B), BF16),
            jax.ShapeDtypeStruct((H, B), BF16),
        ),
        in_specs=[
            pl.BlockSpec(memory_space=pltpu.HBM),
            pl.BlockSpec(memory_space=pltpu.HBM),
            pl.BlockSpec(memory_space=pltpu.SMEM),
        ],
        out_specs=(
            pl.BlockSpec(memory_space=pltpu.VMEM),
            pl.BlockSpec(memory_space=pltpu.VMEM),
        ),
        scratch_shapes=[
            pltpu.VMEM((2 * R, 2 * B), BF16),
            pltpu.VMEM((1, R), BF16),
            pltpu.VMEM((8, R), F32),
            pltpu.VMEM((8, R), F32),
            pltpu.VMEM((2 * R, 128), F32),
            pltpu.VMEM((B, R), BF16),
            pltpu.VMEM((H, 2 * R), BF16),
            pltpu.VMEM((H, B), F32),
            pltpu.VMEM((tiles, Q), BF16),
            pltpu.VMEM((tiles, Q), BF16),
            pltpu.VMEM((tiles, Q), BF16),
            pltpu.VMEM((tiles, Q), BF16),
            pltpu.VMEM((2 * Q, Q), BF16),
            pltpu.SemaphoreType.DMA((6,)),
            pltpu.SemaphoreType.DMA((5,)),
            pltpu.SemaphoreType.DMA((5,)),
            pltpu.SemaphoreType.DMA((5,)),
            pltpu.SemaphoreType.DMA((5,)),
            pltpu.SemaphoreType.DMA((6,)),
            pltpu.SemaphoreType.DMA((6,)),
            pltpu.SemaphoreType.DMA((2,)),
            pltpu.SemaphoreType.DMA((2,)),
        ],
        compiler_params=pltpu.CompilerParams(
            collective_id=0, has_side_effects=True, vmem_limit_bytes=VMEM_BYTES
        ),
        cost_estimate=pl.CostEstimate(
            flops=flops, bytes_accessed=4 * R * B * 2 + 4 * H * B, transcendentals=0
        ),
    )(in_hbm(panels), in_hbm(barrier), counts)
    return diag[None], cross[None]


def solution(mesh):
    return jax.shard_map(
        body,
        mesh=mesh,
        in_specs=(
            P(("scen", "tm"), "panel", None),
            P(("scen", "tm"), "panel"),
            P(("scen", "tm"), "panel"),
        ),
        out_specs=(P(("scen", "tm"), "panel", None), P(("scen", "tm"), "panel", None)),
        check_vma=False,
    )
```

```python
import functools

import jax
import jax.numpy as jnp
from jax import lax
from jax.experimental import pallas as pl
from jax.experimental.pallas import tpu as pltpu
from jax.sharding import PartitionSpec as P

PR = 64
VMEM_BYTES = 48 * 1024 * 1024
MESH = pl.DeviceIdType.MESH
F32 = jnp.float32
BF16 = jnp.bfloat16
PAD = 16


def gram(left, right):
    return jnp.dot(left, right, preferred_element_type=F32)


def kernel(
    blocks,
    panels_ref,
    barrier_ref,
    counts_ref,
    diag_ref,
    cross_ref,
    rows,
    diagonal_row,
    weight_row,
    weight_peer,
    weight_col,
    right_t,
    left_t,
    total,
    part_out,
    part_in,
    out_tiles,
    in_tiles,
    peer_tiles,
    local_sem,
    peer_send,
    peer_recv,
    part_send,
    part_recv,
    link_send,
    link_recv,
    pass_send,
    pass_recv,
):
    R = panels_ref.shape[1]
    B = panels_ref.shape[2] // 2
    H = B // 2
    Q = H // 2
    E = Q // 2
    s, t, p = lax.axis_index("scen"), lax.axis_index("tm"), lax.axis_index("panel")
    q = 1 - p
    peer = (s, t, q)
    after = (s, lax.rem(t + 1, blocks), p)
    before = (s, lax.rem(t + blocks - 1, blocks), p)
    has_before, has_after = t > 0, t < blocks - 1

    def right_tile(half, tile):
        return pl.ds(pl.multiple_of(B + half * H + tile * Q, Q), Q)

    def local(columns, which):
        return pltpu.make_async_copy(
            panels_ref.at[0, :, columns], rows.at[pl.ds(0, R), columns], local_sem.at[which]
        )

    diagonal_copy = pltpu.make_async_copy(barrier_ref, diagonal_row, local_sem.at[5])
    diagonal_copy.start()
    local_right = [
        local(right_tile(q, 0), 0),
        local(right_tile(p, q), 1),
        local(right_tile(q, 1), 2),
        local(right_tile(p, p), 3),
    ]
    local_left = local(pl.ds(0, B), 4)
    for copy in local_right[:2]:
        copy.start()

    entry = pltpu.get_barrier_semaphore()
    pl.semaphore_signal(entry, inc=1, device_id=peer, device_id_type=MESH)

    @pl.when(has_before)
    def _():
        pl.semaphore_signal(entry, inc=1, device_id=before, device_id_type=MESH)

    @pl.when(has_after)
    def _():
        pl.semaphore_signal(entry, inc=1, device_id=after, device_id_type=MESH)

    spot = lax.broadcasted_iota(jnp.int32, (8, R), 1)
    diagonal_copy.wait()
    diagonal = jnp.broadcast_to(diagonal_row[...].astype(F32), (8, R))
    weight_row[...] = jnp.where(spot < counts_ref[0, 0] * PR, diagonal, 0.0)

    def to_peer(columns, which):
        return pltpu.make_async_remote_copy(
            src_ref=panels_ref.at[0, :, columns],
            dst_ref=rows.at[pl.ds(R, R), columns],
            send_sem=peer_send.at[which],
            recv_sem=peer_recv.at[which],
            device_id=peer,
            device_id_type=MESH,
        )

    def exchange(dest):
        return [
            to_peer(pl.ds(pl.multiple_of(dest * H, H), H), 0),
            to_peer(pl.ds(pl.multiple_of((1 - dest) * H, H), H), 1),
            to_peer(pl.ds(B, H), 2),
            to_peer(pl.ds(B + H, H), 3),
        ]

    sent = exchange(q)
    came = exchange(p)

    weight_copy = pltpu.make_async_remote_copy(
        src_ref=weight_row,
        dst_ref=weight_peer,
        send_sem=peer_send.at[4],
        recv_sem=peer_recv.at[4],
        device_id=peer,
        device_id_type=MESH,
    )
    def spread(row):
        return jnp.broadcast_to(row[0:1, :], (128, R)).T

    def scaled_t(group, columns, width):
        weight = weight_col[pl.ds(group * R, R), :]
        plain = rows[pl.ds(group * R, R), columns].astype(F32)
        weight = jnp.concatenate([weight] * (width // 128), axis=1)
        return (plain * weight).astype(BF16).T

    def link(first, length, which):
        return pltpu.make_async_remote_copy(
            src_ref=out_tiles.at[pl.ds(first, length), :],
            dst_ref=in_tiles.at[pl.ds(first, length), :],
            send_sem=link_send.at[which],
            recv_sem=link_recv.at[which],
            device_id=after,
            device_id_type=MESH,
        )

    links = [
        link(0, E, 0),
        link(Q, Q, 1),
        link(2 * Q, Q + PAD, 2),
        link(3 * Q + PAD, E, 3),
        link(3 * Q + PAD + E, E, 4),
        link(E, E, 5),
    ]

    def send_on(which):
        @pl.when(has_after)
        def _():
            links[which].start()

    lower = lax.broadcasted_iota(jnp.int32, (Q, Q), 0)
    upper = lax.broadcasted_iota(jnp.int32, (Q, Q), 1)

    def part(first, length, which):
        return pltpu.make_async_remote_copy(
            src_ref=part_out.at[pl.ds(first, length), :],
            dst_ref=part_in.at[pl.ds(first, length), :],
            send_sem=part_send.at[which],
            recv_sem=part_recv.at[which],
            device_id=peer,
            device_id_type=MESH,
        )

    parts = [
        part(0, E, 0),
        part(Q, Q, 1),
        part(2 * Q, Q + PAD, 2),
        part(3 * Q + PAD, Q, 3),
        part(E, E, 4),
    ]

    def turn(dest, tile):
        half = q if dest else p
        right_t[pl.ds((2 - 2 * dest + tile) * Q, Q), :] = scaled_t(0, right_tile(half, tile), Q)

    def side(dest, tile):
        return right_t[pl.ds((2 - 2 * dest + tile) * Q, Q), :]

    def own(columns):
        return rows[pl.ds(0, R), columns]

    def across_tile(dest, tile):
        home, away = (q, p) if dest else (p, q)
        return gram(side(dest, tile), own(right_tile(away, lax.rem(tile + home, 2))))

    def packed_tile(dest):
        home = q if dest else p
        first = gram(side(dest, 0), own(right_tile(home, 0)))
        second = gram(side(dest, 1), own(right_tile(home, 1)))
        middle = jnp.sum(jnp.where(upper == lower, second, 0.0), axis=0, keepdims=True)
        return jnp.where(upper >= lower, first, second), jnp.broadcast_to(middle, (PAD, Q))

    def square_tile(dest):
        home = q if dest else p
        return gram(side(dest, 0), own(right_tile(home, 1)))

    weight_col[pl.ds(0, R), :] = spread(weight_row[...])
    local_right[0].wait()
    turn(1, 0)
    local_right[1].wait()
    for copy in local_right[2:]:
        copy.start()
    local_left.start()
    part_out[pl.ds(0, Q), :] = across_tile(1, 0).astype(BF16)
    pl.semaphore_wait(entry, 1 + has_before.astype(jnp.int32) + has_after.astype(jnp.int32))
    parts[0].start()
    parts[4].start()
    local_right[2].wait()
    local_right[3].wait()
    turn(0, 0)
    mine = across_tile(0, 0)
    parts[0].wait_recv()
    out_tiles[pl.ds(0, E), :] = (mine[:E] + part_in[pl.ds(0, E), :].astype(F32)).astype(BF16)
    send_on(0)
    parts[4].wait_recv()
    out_tiles[pl.ds(E, E), :] = (mine[E:] + part_in[pl.ds(E, E), :].astype(F32)).astype(BF16)
    send_on(5)

    turn(1, 1)
    part_out[pl.ds(Q, Q), :] = across_tile(1, 1).astype(BF16)
    parts[1].start()
    weight_copy.start()
    sent[0].start()
    sent[1].start()
    packed, middle = packed_tile(1)
    part_out[pl.ds(2 * Q, Q), :] = packed.astype(BF16)
    part_out[pl.ds(3 * Q, PAD), :] = middle.astype(BF16)
    parts[2].start()
    part_out[pl.ds(3 * Q + PAD, Q), :] = square_tile(1).astype(BF16)
    parts[3].start()
    sent[2].start()
    sent[3].start()

    turn(0, 1)
    mine = across_tile(0, 1)
    parts[1].wait_recv()
    out_tiles[pl.ds(Q, Q), :] = (mine + part_in[pl.ds(Q, Q), :].astype(F32)).astype(BF16)
    send_on(1)

    packed, middle = packed_tile(0)
    parts[2].wait_recv()
    out_tiles[pl.ds(2 * Q, Q), :] = (
        packed + part_in[pl.ds(2 * Q, Q), :].astype(F32)
    ).astype(BF16)
    out_tiles[pl.ds(3 * Q, PAD), :] = (
        middle + part_in[pl.ds(3 * Q, PAD), :].astype(F32)
    ).astype(BF16)
    send_on(2)
    mine = square_tile(0)
    parts[3].wait_recv()
    out_tiles[pl.ds(3 * Q + PAD, Q), :] = (
        mine + part_in[pl.ds(3 * Q + PAD, Q), :].astype(F32)
    ).astype(BF16)
    send_on(3)
    send_on(4)

    weight_copy.wait_recv()
    weight_col[pl.ds(R, R), :] = spread(weight_peer[...])
    own_left = pl.ds(pl.multiple_of(p * H, H), H)
    local_left.wait()
    left_t[:, pl.ds(0, R)] = scaled_t(0, own_left, H)
    came[0].wait_recv()
    left_t[:, pl.ds(R, R)] = scaled_t(1, own_left, H)
    came[1].wait_recv()

    def left_step(step, carry):
        here = pl.ds(pl.multiple_of(step * Q, Q), Q)
        total[:, here] = gram(left_t[...], rows[:, here])
        return carry

    lax.fori_loop(0, B // Q, left_step, 0)

    def cross_step(step, carry):
        here = pl.ds(pl.multiple_of(step * Q, Q), Q)
        there = pl.ds(pl.multiple_of(B + step * Q, Q), Q)
        cross_ref[:, here] = gram(left_t[...], rows[:, there]).astype(BF16)
        return carry

    def handed(which):
        return pltpu.make_async_remote_copy(
            src_ref=in_tiles.at[pl.ds(which * Q, Q), :],
            dst_ref=peer_tiles.at[pl.ds(which * Q, Q), :],
            send_sem=pass_send.at[which],
            recv_sem=pass_recv.at[which],
            device_id=peer,
            device_id_type=MESH,
        )

    passes = [handed(0), handed(1)]

    @pl.when(has_before)
    def _():
        links[0].wait_recv()
        links[5].wait_recv()
        passes[0].start()

    came[2].wait_recv()
    came[3].wait_recv()
    lax.fori_loop(0, B // Q, cross_step, 0)

    def columns(half, tile):
        return pl.ds(pl.multiple_of(half * H + tile * Q, Q), Q)

    def band(tile):
        return pl.ds(pl.multiple_of(tile * Q, Q), Q)

    def put(row_tile, where, value):
        diag_ref[band(row_tile), where] = (total[band(row_tile), where] + value).astype(BF16)

    @pl.when(t == 0)
    def _():
        diag_ref[...] = total[...].astype(BF16)

    @pl.when(has_before)
    def _():
        put(0, columns(q, p), in_tiles[pl.ds(0, Q), :].astype(F32))
        links[1].wait_recv()
        passes[1].start()
        put(1, columns(q, 1 - p), in_tiles[pl.ds(Q, Q), :].astype(F32))
        for tile in range(2):
            passes[tile].wait_recv()
            turned = peer_tiles[pl.ds(tile * Q, Q), :].astype(F32).T
            put(lax.rem(tile + q, 2), columns(q, tile), turned)
        links[2].wait_recv()
        packed = in_tiles[pl.ds(2 * Q, Q), :].astype(F32)
        turned = packed.T
        put(0, columns(p, 0), jnp.where(upper >= lower, packed, turned))
        middle_row = in_tiles[pl.ds(3 * Q, PAD), :].astype(F32)[0:1, :]
        put(
            1,
            columns(p, 1),
            jnp.where(
                upper == lower,
                jnp.broadcast_to(middle_row, (Q, Q)),
                jnp.where(upper < lower, packed, turned),
            ),
        )
        for part in range(2):
            links[3 + part].wait_recv()
            piece = in_tiles[pl.ds(3 * Q + PAD + part * E, E), :].astype(F32)
            across = pl.ds(part * E, E)
            diag_ref[across, columns(p, 1)] = (total[across, columns(p, 1)] + piece).astype(BF16)
            down = pl.ds(pl.multiple_of(p * H + part * E, E), E)
            diag_ref[pl.ds(Q, Q), down] = (total[pl.ds(Q, Q), down] + piece.T).astype(BF16)
        for copy in passes:
            copy.wait_send()

    weight_copy.wait_send()
    for copy in sent + parts:
        copy.wait_send()

    @pl.when(has_after)
    def _():
        for copy in links:
            copy.wait_send()


def in_hbm(array):
    return pltpu.with_memory_space_constraint(array, pltpu.HBM)


def body(panels, barrier, counts):
    R = panels.shape[1]
    B = panels.shape[2] // 2
    H = B // 2
    Q = H // 2
    tiles = 4 * Q + PAD
    flops = 2 * 3 * H * B * 2 * R
    diag, cross = pl.pallas_call(
        functools.partial(kernel, lax.axis_size("tm")),
        out_shape=(
            jax.ShapeDtypeStruct((H, B), BF16),
            jax.ShapeDtypeStruct((H, B), BF16),
        ),
        in_specs=[
            pl.BlockSpec(memory_space=pltpu.HBM),
            pl.BlockSpec(memory_space=pltpu.HBM),
            pl.BlockSpec(memory_space=pltpu.SMEM),
        ],
        out_specs=(
            pl.BlockSpec(memory_space=pltpu.VMEM),
            pl.BlockSpec(memory_space=pltpu.VMEM),
        ),
        scratch_shapes=[
            pltpu.VMEM((2 * R, 2 * B), BF16),
            pltpu.VMEM((1, R), BF16),
            pltpu.VMEM((8, R), F32),
            pltpu.VMEM((8, R), F32),
            pltpu.VMEM((2 * R, 128), F32),
            pltpu.VMEM((B, R), BF16),
            pltpu.VMEM((H, 2 * R), BF16),
            pltpu.VMEM((H, B), F32),
            pltpu.VMEM((tiles, Q), BF16),
            pltpu.VMEM((tiles, Q), BF16),
            pltpu.VMEM((tiles, Q), BF16),
            pltpu.VMEM((tiles, Q), BF16),
            pltpu.VMEM((2 * Q, Q), BF16),
            pltpu.SemaphoreType.DMA((6,)),
            pltpu.SemaphoreType.DMA((5,)),
            pltpu.SemaphoreType.DMA((5,)),
            pltpu.SemaphoreType.DMA((5,)),
            pltpu.SemaphoreType.DMA((5,)),
            pltpu.SemaphoreType.DMA((6,)),
            pltpu.SemaphoreType.DMA((6,)),
            pltpu.SemaphoreType.DMA((2,)),
            pltpu.SemaphoreType.DMA((2,)),
        ],
        compiler_params=pltpu.CompilerParams(
            collective_id=0, has_side_effects=True, vmem_limit_bytes=VMEM_BYTES
        ),
        cost_estimate=pl.CostEstimate(
            flops=flops, bytes_accessed=4 * R * B * 2 + 4 * H * B, transcendentals=0
        ),
    )(in_hbm(panels), in_hbm(barrier), counts)
    return diag[None], cross[None]


def solution(mesh):
    return jax.shard_map(
        body,
        mesh=mesh,
        in_specs=(
            P(("scen", "tm"), "panel", None),
            P(("scen", "tm"), "panel"),
            P(("scen", "tm"), "panel"),
        ),
        out_specs=(P(("scen", "tm"), "panel", None), P(("scen", "tm"), "panel", None)),
        check_vma=False,
    )
```
